512 devices in a mesh: chain: 32 (over z, core), bond: 16 (over y, x).
Axes of the slice: x: 4, y: 4, z: 16, core: 2. Of those that a mesh axis runs over, the one named last changes fastest.
Arguments:
- sites: bfloat16 [32, 1024, 2048], P('chain', 'bond'), may hold values from -0.1875 to 0.1875
- start: bfloat16 [32, 1024, 1024], P('chain', 'bond'), may hold values from -0.125 to 0.125
- gates: float32 [32, 16], replicated, may hold values from -3 to 3
- bonds: int32 [33], replicated, may hold values from 512 to 1024, as said below
Outputs:
- new_sites: float32 [32, 1024, 2048], P('chain', 'bond')
The draws below stay inside these ranges and needn't reach their ends.
Inputs may be any that keep to these rules, and one draw needn't show every extreme that they name: bonds[k] is the bond dimension of the cut just left of site k.
All inputs are finite; a program needn't handle non-finite values.
Results may differ from the reference program's by a relative error of at most 0.03.
Values may be sent and summed in bfloat16 or wider, within the bound.
No kernel may reach another device: no remote copies, remote signals or barrier semaphores. Data moves between devices by JAX's collectives and lax.ppermute only.
A program may use at most 128 MiB of HBM per device.

```python
import jax
import jax.numpy as jnp
from jax import lax

CHI = 1024
SITES = 32
N_BOND = 16


def draw_bonds(key, part):
    values = jax.random.randint(key, (SITES + 1,), CHI // 2, CHI + 1).astype(jnp.int32)
    values = values.at[0].set(CHI // 2)
    return values.at[SITES // 2].set(CHI)


def levels(key, shape, shards, smallest, top_value):
    factor_of, own = 1.0, jax.random.fold_in(key, 6)
    for position, parts in shards:
        heights = jnp.exp(jax.random.uniform(jax.random.fold_in(own, position), (parts,), jnp.float32, smallest / len(shards), top_value / len(shards)))
        factor_of = factor_of * jnp.repeat(heights, shape[position] // parts).reshape([-1 if axis == position else 1 for axis in range(len(shape))])
    return factor_of


def noise(key, dims, width, limit, cuts=(), held_as=jnp.bfloat16):
    drawn = jax.random.normal(key, dims, jnp.float32) * width
    if len(cuts) > 0:
        drawn = levels(key, dims, cuts, -0.22, 0.18) * drawn
    return jnp.clip(drawn, min=-limit, max=limit).astype(held_as)


def setup_inputs(seed: int = 0) -> dict:
    key_of = jax.random.split(jax.random.key(seed), 5)
    return {
        "sites": noise(key_of[0], (SITES, CHI, 2 * CHI), CHI ** -0.5, 0.1875, ((0, 32), (1, 16))),
        "start": noise(key_of[1], (SITES, CHI, CHI), (2 * CHI) ** -0.5, 0.125, ((0, 32), (1, 16))),
        "gates": noise(key_of[2], (SITES, 16), 0.5, 3.0, (), jnp.float32),
        "bonds": draw_bonds(jax.random.fold_in(key_of[4], 71), 0),
    }


ridge_ratio = 0.05

def pair_update(left_tensor, right_tensor, start_low, start_high, gate_row, bond_left, bond_mid, bond_right):
    columns = jnp.arange(CHI)
    mid_keep = columns < bond_mid
    right_keep = columns < bond_right
    left_keep = (columns < bond_left)[:, None] & jnp.tile(mid_keep, 2)[None, :]
    left_used = jnp.where(left_keep, left_tensor, jnp.zeros((), jnp.bfloat16))
    right_used = jnp.where(jnp.tile(right_keep, 2)[None, :], right_tensor, jnp.zeros((), jnp.bfloat16))
    mix_zero = jnp.dot(left_used[:, :CHI].astype(jnp.float32), right_used.astype(jnp.float32), preferred_element_type=jnp.float32)
    mix_one = jnp.dot(left_used[:, CHI:].astype(jnp.float32), right_used.astype(jnp.float32), preferred_element_type=jnp.float32)
    gate_matrix = gate_row.reshape(4, 4)
    theta_list = []
    for out_row in range(2):
        pieces = []
        for out_col in range(2):
            coeffs = gate_matrix[2 * out_row + out_col]
            pieces.append(coeffs[0] * mix_zero[:, :CHI] + coeffs[1] * mix_zero[:, CHI:] + coeffs[2] * mix_one[:, :CHI] + coeffs[3] * mix_one[:, CHI:])
        theta_list.append(jnp.concatenate(pieces, axis=1).astype(jnp.bfloat16))
    basis_start = jnp.where(mid_keep[None, :], jnp.concatenate([start_low, start_high], axis=0), jnp.zeros((), jnp.bfloat16))
    local_rows = CHI // N_BOND
    summed = jnp.zeros((2 * CHI, CHI), jnp.float32)
    for theta_rows in theta_list:
        image_rows = jnp.dot(theta_rows.astype(jnp.float32), basis_start.astype(jnp.float32), preferred_element_type=jnp.float32).astype(jnp.bfloat16)
        split_theta = theta_rows.reshape(N_BOND, local_rows, 2 * CHI).astype(jnp.float32)
        split_image = image_rows.reshape(N_BOND, local_rows, CHI).astype(jnp.float32)
        block_terms = jnp.einsum('kar,kas->krs', split_theta, split_image)
        rounded = lax.optimization_barrier(block_terms.astype(jnp.bfloat16))
        summed = summed + lax.optimization_barrier(jnp.sum(rounded.astype(jnp.float32), axis=0))
    projected = summed
    gram_matrix = lax.dot_general(projected.astype(jnp.float32), projected.astype(jnp.float32), (((0,), (0,)), ((), ())), precision=lax.Precision.HIGHEST, preferred_element_type=jnp.float32)
    trace_sum = jnp.sum(jnp.diagonal(gram_matrix))
    kept_count = jnp.sum(mid_keep.astype(jnp.float32))
    added = jnp.where(mid_keep, ridge_ratio * trace_sum / kept_count, 1.0).astype(jnp.float32)
    factor = jnp.linalg.cholesky(gram_matrix + jnp.diag(added))
    exact_basis = lax.linalg.triangular_solve(factor, projected, left_side=False, lower=True, transpose_a=True)
    basis_new = exact_basis.astype(jnp.bfloat16)
    upper_rows = jnp.concatenate([jnp.dot(theta_rows.astype(jnp.float32), basis_new.astype(jnp.float32), preferred_element_type=jnp.float32) for theta_rows in theta_list], axis=1)
    sum_squares = jnp.sum(upper_rows * upper_rows)
    mean_square = sum_squares / (2.0 * bond_left.astype(jnp.float32) * bond_mid.astype(jnp.float32)) + 1e-06
    new_left = upper_rows * lax.rsqrt(mean_square)
    new_right = jnp.sqrt(2.0 * bond_right.astype(jnp.float32)) * exact_basis.T
    return (new_left, new_right)

def reference(sites, start, gates, bonds):
    updated = jnp.zeros((SITES, CHI, 2 * CHI), jnp.float32)

    def apply_pair(current, pair_index):
        left_site = (2 * pair_index).astype(jnp.int32)
        new_left, new_right = pair_update(sites[left_site], sites[left_site + 1], start[left_site], start[left_site + 1], gates[left_site], bonds[left_site], bonds[left_site + 1], bonds[left_site + 2])
        current = lax.dynamic_update_index_in_dim(current, new_left, left_site, 0)
        current = lax.dynamic_update_index_in_dim(current, new_right, (left_site + 1).astype(jnp.int32), 0)
        return (current, None)
    updated, _ = lax.scan(apply_pair, updated, jnp.arange(SITES // 2).astype(jnp.int32))
    return updated
```

```python
import functools

import jax
import jax.numpy as jnp
from jax import lax
from jax.experimental import pallas as pl
from jax.experimental.pallas import tpu as pltpu
from jax.sharding import Mesh
from jax.sharding import PartitionSpec as P

BOND = ("y", "x")
NB = 128
SB = 16

ridge_ratio = 0.05
bf16 = jnp.bfloat16
f32 = jnp.float32


def split(x):
    high = x.astype(bf16)
    return high, (x - high.astype(f32)).astype(bf16)


def tn3(a, b):
    return lax.dot_general(
        jnp.concatenate([a[0], a[0], a[1]], 0),
        jnp.concatenate([b[0], b[1], b[0]], 0),
        (((0,), (0,)), ((), ())),
        preferred_element_type=f32,
    )


def nn3(a, b):
    return jnp.dot(
        jnp.concatenate([a[0], a[0], a[1]], 1),
        jnp.concatenate([b[0], b[1], b[0]], 0),
        preferred_element_type=f32,
    )


def diag_factor(dm, xs):
    for base in range(0, NB, SB):
        block = dm[pl.ds(base, SB), :NB]
        a = {}
        for k in range(SB):
            for m in range(k + 1):
                a[k, m] = jnp.broadcast_to(block[k : k + 1, base + m : base + m + 1], (1, NB))
        rows = [dm[pl.ds(base + k, 1), :] for k in range(SB)]
        for j in range(SB):
            rinv = lax.rsqrt(a[j, j])
            x = rows[j] * jnp.concatenate([rinv, rinv], 1)
            xs[pl.ds(base + j, 1), :] = x
            col = {k: a[k, j] * rinv for k in range(j + 1, SB)}
            for k in range(j + 1, SB):
                for m in range(j + 1, k + 1):
                    a[k, m] = a[k, m] - col[k] * col[m]
                rows[k] = rows[k] - jnp.concatenate([col[k], col[k]], 1) * x
        end = base + SB
        if end < NB:
            high, low = split(xs[pl.ds(base, SB), :])
            u = tn3((high[:, :NB], low[:, :NB]), (high, low))
            dm[end:, :] = dm[end:, :] - u[end:]


def inverse_factor_kernel(r_ref, g_ref, z, dm, xs):
    n = g_ref.shape[0]
    blocks = n // NB
    r = r_ref[0]
    i0 = lax.broadcasted_iota(jnp.int32, (NB, NB), 0)
    i1 = lax.broadcasted_iota(jnp.int32, (NB, NB), 1)
    eye = i0 == i1
    trace = jnp.zeros((NB, NB), f32)
    for j in range(blocks):
        at = j * NB
        trace = trace + jnp.where(eye, g_ref[at : at + NB, at : at + NB], 0.0)
    added = ridge_ratio * jnp.sum(trace) / r.astype(f32)
    z[...] = g_ref[...]

    def outer(j, carry):
        js = pl.multiple_of(j * NB, NB)
        d = z[pl.ds(js, NB), pl.ds(js, NB)]
        dm[:, :NB] = d + jnp.where(eye, jnp.where(i0 + js < r, added, 1.0), 0.0)
        dm[:, NB:] = jnp.where(eye, 1.0, 0.0)
        diag_factor(dm, xs)
        inv = xs[:, NB:]
        z[pl.ds(js, NB), :] = nn3(split(inv), split(z[pl.ds(js, NB), :]))
        z[pl.ds(js, NB), pl.ds(js, NB)] = inv
        done = split(z[pl.ds(js, NB), :])

        def update(k, carry):
            ks = pl.multiple_of(k * NB, NB)
            u = tn3(split(z[pl.ds(js, NB), pl.ds(ks, NB)]), done)
            z[pl.ds(ks, NB), pl.ds(js, NB)] = jnp.zeros((NB, NB), f32)
            z[pl.ds(ks, NB), :] = z[pl.ds(ks, NB), :] - u
            return carry

        lax.fori_loop(j + 1, blocks, update, 0)
        return carry

    lax.fori_loop(0, blocks, outer, 0)
    for j in range(blocks - 1):
        at = j * NB
        z[at : at + NB, at + NB :] = jnp.zeros((NB, n - at - NB), f32)


def inverse_factor(gram, kept):
    n = gram.shape[0]
    return pl.pallas_call(
        inverse_factor_kernel,
        out_shape=jax.ShapeDtypeStruct((n, n), f32),
        in_specs=[
            pl.BlockSpec(memory_space=pltpu.SMEM),
            pl.BlockSpec(memory_space=pltpu.VMEM),
        ],
        out_specs=pl.BlockSpec(memory_space=pltpu.VMEM),
        scratch_shapes=[pltpu.VMEM((NB, 2 * NB), f32), pltpu.VMEM((NB, 2 * NB), f32)],
        compiler_params=pltpu.CompilerParams(vmem_limit_bytes=40 * 2**20),
        cost_estimate=pl.CostEstimate(
            flops=4 * n**3, bytes_accessed=8 * n * n, transcendentals=n
        ),
    )(kept.reshape(1), gram)


def other_core(value):
    return lax.ppermute(value, "core", [(0, 1), (1, 0)])


def gathered(value, axis_name):
    return lax.all_gather(value, axis_name, axis=0, tiled=True)


def column_gram(values):
    return lax.dot_general(
        values, values, (((0,), (0,)), ((), ())), preferred_element_type=f32
    )


def local(sites, start, gates, bonds):
    core = lax.axis_index("core")
    bond_index = lax.axis_index(BOND)
    is_left = core == 0
    width = start.shape[2]
    rows = sites.shape[1]
    left_site = 2 * lax.axis_index("z")
    bond_left = bonds[left_site]
    bond_mid = bonds[left_site + 1]
    bond_right = bonds[left_site + 2]
    columns = jnp.arange(width)
    mid_keep = columns < bond_mid
    right_keep = columns < bond_right
    row_keep = bond_index * rows + jnp.arange(rows) < bond_left
    own_site = sites[0]
    own_start = start[0]

    other_site = other_core(own_site)
    a_rows = jnp.where(is_left, own_site, other_site)
    b_rows = jnp.where(is_left, other_site[:, :width], own_site[:, width:])
    near = gathered(jnp.concatenate([b_rows, own_start], axis=1), "x")
    b_full = gathered(near[:, :width], "y")
    start_full = gathered(near[:, width:], "y")

    keep = row_keep[:, None] & mid_keep[None, :]
    a_stack = jnp.concatenate(
        [jnp.where(keep, a_rows[:, i * width : (i + 1) * width], jnp.zeros((), bf16)) for i in (0, 1)], 0
    )
    mixed = jnp.where(right_keep[None, :], jnp.dot(a_stack, b_full, preferred_element_type=f32), 0.0)
    gate = gates[left_site].reshape(2, 2, 2, 2)
    gate = lax.dynamic_index_in_dim(gate, core, 3, keepdims=False)

    def mix(q):
        u = lax.dynamic_index_in_dim(gate, q, 1, keepdims=False)
        return jnp.concatenate(
            [u[o, 0] * mixed[:rows] + u[o, 1] * mixed[rows:] for o in (0, 1)], 0
        )

    theta = (mix(core) + other_core(mix(1 - core))).astype(bf16)
    part = jnp.dot(theta, start_full, preferred_element_type=f32)
    image = jnp.where(mid_keep[None, :], part + other_core(part), 0.0).astype(bf16)
    terms = lax.dot_general(
        theta, image, (((0,), (0,)), ((), ())), preferred_element_type=f32
    ).astype(bf16)
    arrived = lax.all_to_all(
        terms.reshape(-1, rows, width), BOND, split_axis=0, concat_axis=0, tiled=True
    )
    projected = arrived.astype(f32).sum(axis=0).astype(bf16)
    own_half = gathered(gathered(projected, "x"), "y")
    other_half = other_core(own_half)
    other_theta = other_core(theta)

    gram = column_gram(own_half) + column_gram(other_half)
    inverse = inverse_factor(gram, bond_mid)
    carried = jnp.dot(theta, own_half, preferred_element_type=f32) + jnp.dot(
        other_theta, other_half, preferred_element_type=f32
    )
    upper = lax.dot_general(
        carried,
        inverse,
        (((1,), (1,)), ((), ())),
        precision=lax.Precision.HIGHEST,
        preferred_element_type=f32,
    )
    sum_squares = lax.psum(lax.psum(jnp.sum(upper * upper), "x"), "y")
    mean_square = sum_squares / (2.0 * bond_left.astype(f32) * bond_mid.astype(f32)) + 1e-06
    new_left = jnp.concatenate([upper[:rows], upper[rows:]], 1) * lax.rsqrt(mean_square)

    scale = jnp.sqrt(2.0 * bond_right.astype(f32))
    part_high, part_low = split(
        lax.dynamic_slice_in_dim(inverse, bond_index * rows, rows, 0) * scale
    )
    both = jnp.concatenate([part_high, part_low], 0)

    def right_half(half):
        value = lax.dot_general(both, half, (((1,), (1,)), ((), ())), preferred_element_type=f32)
        return value[:rows] + value[rows:]

    new_right = jnp.concatenate([right_half(other_half), right_half(own_half)], 1)
    return jnp.where(is_left, new_left, new_right)[None]


def solution(mesh):
    chain, bond = mesh.shape["chain"], mesh.shape["bond"]
    side = 4
    torus = Mesh(
        mesh.devices.reshape(chain // 2, 2, bond // side, side), ("z", "core", "y", "x")
    )
    whole = P(("z", "core"), BOND, None)
    return jax.shard_map(
        local, mesh=torus, in_specs=(whole, whole, P(), P()), out_specs=whole, check_vma=False
    )
```

```python
import functools

import jax
import jax.numpy as jnp
from jax import lax
from jax.experimental import pallas as pl
from jax.experimental.pallas import tpu as pltpu
from jax.sharding import Mesh
from jax.sharding import PartitionSpec as P

BOND = ("y", "x")
NB = 128
SB = 32

ridge_ratio = 0.05
bf16 = jnp.bfloat16
f32 = jnp.float32


def split(x):
    high = x.astype(bf16)
    return high, (x - high.astype(f32)).astype(bf16)


def tn3(a, b):
    return lax.dot_general(
        jnp.concatenate([a[0], a[0], a[1]], 0),
        jnp.concatenate([b[0], b[1], b[0]], 0),
        (((0,), (0,)), ((), ())),
        preferred_element_type=f32,
    )


def nn3(a, b):
    return jnp.dot(
        jnp.concatenate([a[0], a[0], a[1]], 1),
        jnp.concatenate([b[0], b[1], b[0]], 0),
        preferred_element_type=f32,
    )


def diag_factor(dm, xs):
    groups = SB // 8
    tiles = range(2)
    for base in range(0, NB, SB):
        block = [dm[base + 8 * g : base + 8 * g + 8, :] for g in range(groups)]
        cols = {
            (m, g): jnp.broadcast_to(block[g][:, base + m : base + m + 1], (8, NB))
            for m in range(SB)
            for g in range(m // 8, groups)
        }
        rest = [[block[g][:, t * NB : (t + 1) * NB] for t in tiles] for g in range(groups)]
        for j in range(SB):
            first, sub = divmod(j, 8)
            rinv = lax.rsqrt(jnp.broadcast_to(cols[j, first][sub : sub + 1, :], (8, NB)))
            low = {g: cols[j, g] * rinv for g in range(first, groups)}
            done = [jnp.broadcast_to(rest[first][t][sub : sub + 1, :], (8, NB)) * rinv for t in tiles]
            for t in tiles:
                xs[base + j : base + j + 1, t * NB : (t + 1) * NB] = done[t][0:1, :]
            for m in range(j + 1, SB):
                factor = jnp.broadcast_to(low[m // 8][m % 8 : m % 8 + 1, :], (8, NB))
                for g in range(m // 8, groups):
                    cols[m, g] = cols[m, g] - low[g] * factor
            for g in range(first, groups):
                for t in tiles:
                    rest[g][t] = rest[g][t] - low[g] * done[t]
        end = base + SB
        if end < NB:
            high, rem = split(xs[base:end, :])
            u = tn3((high[:, :NB], rem[:, :NB]), (high, rem))
            dm[end:, :] = dm[end:, :] - u[end:]


def tn(a, b):
    return lax.dot_general(a, b, (((0,), (0,)), ((), ())), preferred_element_type=f32)


def nt(a, b):
    return lax.dot_general(a, b, (((1,), (1,)), ((), ())), preferred_element_type=f32)


def factor_kernel(at_ref, scale_ref, own, other, carried, out, lh, ll, rh, rl, acc, dm, xs):
    n = own.shape[1]
    blocks = n // NB
    r = at_ref[2]
    i0 = lax.broadcasted_iota(jnp.int32, (NB, NB), 0)
    i1 = lax.broadcasted_iota(jnp.int32, (NB, NB), 1)
    lanes = lax.broadcasted_iota(jnp.int32, (NB, n), 1)
    eye = i0 == i1
    squares = jnp.zeros((NB, n), f32)
    for p in (own, other):
        for at in range(0, p.shape[0], NB):
            value = p[at : at + NB, :].astype(f32)
            squares = squares + value * value
    added = ridge_ratio * jnp.sum(squares) / r.astype(f32)

    def outer(j, carry):
        js = pl.multiple_of(j * NB, NB)
        for block in range(blocks):

            @pl.when(j == block)
            def _(at=block * NB):
                here = slice(at, at + NB)
                g = tn(own[:, here], own[:, at:]) + tn(other[:, here], other[:, at:])
                if at:
                    h, l = rh[:at, here], rl[:at, here]
                    g = g - (tn(h, rh[:at, at:]) + tn(h, rl[:at, at:]) + tn(l, rh[:at, at:]))
                    acc[:, :at] = -(tn(h, lh[:at, :at]) + tn(h, ll[:at, :at]) + tn(l, lh[:at, :at]))
                acc[:, at:] = g

        d = acc[:, pl.ds(js, NB)]
        dm[:, :NB] = d + jnp.where(eye, jnp.where(i0 + js < r, added, 1.0), 0.0)
        dm[:, NB:] = jnp.where(eye, 1.0, 0.0)
        diag_factor(dm, xs)
        inv = split(xs[:, NB:])
        row = nn3(inv, split(acc[...]))
        rh[pl.ds(js, NB), :], rl[pl.ds(js, NB), :] = split(row)
        lh[pl.ds(js, NB), :], ll[pl.ds(js, NB), :] = split(jnp.where(lanes < js, row, 0.0))
        lh[pl.ds(js, NB), pl.ds(js, NB)], ll[pl.ds(js, NB), pl.ds(js, NB)] = inv
        return carry

    lax.fori_loop(0, blocks, outer, 0)
    rows = out.shape[0]
    left = at_ref[0] == 0

    @pl.when(left)
    def _():
        high, low = split(carried[...])
        upper = nt(high, lh[...]) + nt(low, lh[...]) + nt(high, ll[...])
        out[:, :n] = upper[:rows]
        out[:, n:] = upper[rows:]

    @pl.when(jnp.logical_not(left))
    def _():
        at = pl.multiple_of(at_ref[1] * rows, rows)
        both = jnp.concatenate([lh[pl.ds(at, rows), :], ll[pl.ds(at, rows), :]], 0)
        for q, half in enumerate((other, own)):
            value = nt(both, half[...])
            out[:, q * n : (q + 1) * n] = (value[:rows] + value[rows:]) * scale_ref[0]


def factored(place, scale, own, other, carried):
    n = own.shape[1]
    rows = carried.shape[0] // 2
    smem = pl.BlockSpec(memory_space=pltpu.SMEM)
    vmem = pl.BlockSpec(memory_space=pltpu.VMEM)
    return pl.pallas_call(
        factor_kernel,
        out_shape=(jax.ShapeDtypeStruct((rows, 2 * n), f32), jax.ShapeDtypeStruct((n, n), bf16)),
        in_specs=[smem, smem, vmem, vmem, vmem],
        out_specs=(vmem, vmem),
        scratch_shapes=[
            pltpu.VMEM((n, n), bf16),
            pltpu.VMEM((n, n), bf16),
            pltpu.VMEM((n, n), bf16),
            pltpu.VMEM((NB, n), f32),
            pltpu.VMEM((NB, 2 * NB), f32),
            pltpu.VMEM((NB, 2 * NB), f32),
        ],
        compiler_params=pltpu.CompilerParams(vmem_limit_bytes=32 * 2**20),
        cost_estimate=pl.CostEstimate(
            flops=20 * n**3, bytes_accessed=8 * n * n, transcendentals=n
        ),
    )(place, scale, own, other, carried)


def squares_kernel(lh, shares, total):
    n = lh.shape[0]
    part = jnp.zeros((8, 2 * NB), f32)
    for at in range(0, n, 2 * NB):
        end = at + 2 * NB
        value = nt(shares[:, :end], lh[at:end, :end])
        part = part + (value * value).reshape(-1, 8, 2 * NB).sum(axis=0)
    total[...] = part


def sum_of_squares(lh, shares):
    n = lh.shape[0]
    vmem = pl.BlockSpec(memory_space=pltpu.VMEM)
    return pl.pallas_call(
        squares_kernel,
        out_shape=jax.ShapeDtypeStruct((8, 2 * NB), f32),
        in_specs=[vmem, vmem],
        out_specs=vmem,
        compiler_params=pltpu.CompilerParams(vmem_limit_bytes=24 * 2**20),
        cost_estimate=pl.CostEstimate(flops=n**3, bytes_accessed=4 * n * n, transcendentals=0),
    )(lh, shares)


def other_core(value):
    return lax.ppermute(value, "core", [(0, 1), (1, 0)])


def gathered(value):
    count = lax.axis_size("y") * lax.axis_size("x")
    copies = jnp.broadcast_to(value[None], (count,) + value.shape)
    arrived = lax.all_to_all(copies, BOND, split_axis=0, concat_axis=0, tiled=True)
    return arrived.reshape(count * value.shape[0], value.shape[1])


def local(sites, start, gates, bonds):
    core = lax.axis_index("core")
    bond_index = lax.axis_index(BOND)
    is_left = core == 0
    width = start.shape[2]
    rows = sites.shape[1]
    left_site = 2 * lax.axis_index("z")
    bond_left = bonds[left_site]
    bond_mid = bonds[left_site + 1]
    bond_right = bonds[left_site + 2]
    columns = jnp.arange(width)
    mid_keep = columns < bond_mid
    right_keep = columns < bond_right
    row_keep = bond_index * rows + jnp.arange(rows) < bond_left
    own_site = sites[0]
    own_start = start[0]

    other_site = other_core(own_site)
    a_rows = jnp.where(is_left, own_site, other_site)
    b_rows = jnp.where(is_left, other_site[:, :width], own_site[:, width:])
    b_full = gathered(b_rows)
    start_full = gathered(own_start)

    keep = row_keep[:, None] & mid_keep[None, :]
    a_stack = jnp.concatenate(
        [jnp.where(keep, a_rows[:, i * width : (i + 1) * width], jnp.zeros((), bf16)) for i in (0, 1)], 0
    )
    mixed = jnp.where(right_keep[None, :], jnp.dot(a_stack, b_full, preferred_element_type=f32), 0.0)
    gate = gates[left_site].reshape(2, 2, 2, 2)
    gate = lax.dynamic_index_in_dim(gate, core, 3, keepdims=False)

    def mix(q):
        u = lax.dynamic_index_in_dim(gate, q, 1, keepdims=False)
        return jnp.concatenate(
            [u[o, 0] * mixed[:rows] + u[o, 1] * mixed[rows:] for o in (0, 1)], 0
        )

    theta = (mix(core) + other_core(mix(1 - core))).astype(bf16)
    other_theta, start_full = lax.optimization_barrier((other_core(theta), start_full))
    part = jnp.dot(theta, start_full, preferred_element_type=f32)
    image = jnp.where(mid_keep[None, :], part + other_core(part), 0.0).astype(bf16)
    terms = lax.dot_general(
        theta, image, (((0,), (0,)), ((), ())), preferred_element_type=f32
    ).astype(bf16)
    arrived = lax.all_to_all(
        terms.reshape(-1, rows, width), BOND, split_axis=0, concat_axis=0, tiled=True
    )
    projected = arrived.astype(f32).sum(axis=0).astype(bf16)
    own_half = gathered(projected)
    other_half = other_core(own_half)
    carried = jnp.dot(theta, own_half, preferred_element_type=f32) + jnp.dot(
        other_theta, other_half, preferred_element_type=f32
    )
    share = lax.dynamic_slice_in_dim(carried, core * rows, rows, 0).astype(bf16)
    shares = gathered(share)
    place = jnp.stack([core, bond_index, bond_mid])
    scale = jnp.sqrt(2.0 * bond_right.astype(f32))
    value, lh = factored(place, scale.reshape(1), own_half, other_half, carried)
    share_sum = sum_of_squares(lh, shares)
    total = jnp.sum(share_sum + other_core(share_sum))
    mean_square = total / (2.0 * bond_left.astype(f32) * bond_mid.astype(f32)) + 1e-06
    return (value * jnp.where(is_left, lax.rsqrt(mean_square), 1.0))[None]


def solution(mesh):
    chain, bond = mesh.shape["chain"], mesh.shape["bond"]
    side = 4
    torus = Mesh(
        mesh.devices.reshape(chain // 2, 2, bond // side, side), ("z", "core", "y", "x")
    )
    whole = P(("z", "core"), BOND, None)
    return jax.shard_map(
        local, mesh=torus, in_specs=(whole, whole, P(), P()), out_specs=whole, check_vma=False
    )
```

```python
import functools

import jax
import jax.numpy as jnp
from jax import lax
from jax.experimental import pallas as pl
from jax.experimental.pallas import tpu as pltpu
from jax.sharding import Mesh
from jax.sharding import PartitionSpec as P

BOND = ("y", "x")
NB = 128
SB = 32

ridge_ratio = 0.05
bf16 = jnp.bfloat16
f32 = jnp.float32


def split(x):
    high = x.astype(bf16)
    return high, (x - high.astype(f32)).astype(bf16)


def tn3(a, b):
    return lax.dot_general(
        jnp.concatenate([a[0], a[0], a[1]], 0),
        jnp.concatenate([b[0], b[1], b[0]], 0),
        (((0,), (0,)), ((), ())),
        preferred_element_type=f32,
    )


def nn3(a, b):
    return jnp.dot(
        jnp.concatenate([a[0], a[0], a[1]], 1),
        jnp.concatenate([b[0], b[1], b[0]], 0),
        preferred_element_type=f32,
    )


def diag_factor(dm, xs):
    groups = SB // 8
    tiles = range(2)
    for base in range(0, NB, SB):
        block = [dm[base + 8 * g : base + 8 * g + 8, :] for g in range(groups)]
        cols = {
            (m, g): jnp.broadcast_to(block[g][:, base + m : base + m + 1], (8, NB))
            for m in range(SB)
            for g in range(m // 8, groups)
        }
        rest = [[block[g][:, t * NB : (t + 1) * NB] for t in tiles] for g in range(groups)]
        for j in range(SB):
            first, sub = divmod(j, 8)
            rinv = lax.rsqrt(jnp.broadcast_to(cols[j, first][sub : sub + 1, :], (8, NB)))
            low = {g: cols[j, g] * rinv for g in range(first, groups)}
            done = [jnp.broadcast_to(rest[first][t][sub : sub + 1, :], (8, NB)) * rinv for t in tiles]
            for t in tiles:
                xs[base + j : base + j + 1, t * NB : (t + 1) * NB] = done[t][0:1, :]
            for m in range(j + 1, SB):
                factor = jnp.broadcast_to(low[m // 8][m % 8 : m % 8 + 1, :], (8, NB))
                for g in range(m // 8, groups):
                    cols[m, g] = cols[m, g] - low[g] * factor
            for g in range(first, groups):
                for t in tiles:
                    rest[g][t] = rest[g][t] - low[g] * done[t]
        end = base + SB
        if end < NB:
            high, rem = split(xs[base:end, :])
            u = tn3((high[:, :NB], rem[:, :NB]), (high, rem))
            dm[end:, :] = dm[end:, :] - u[end:]


def tn(a, b):
    return lax.dot_general(a, b, (((0,), (0,)), ((), ())), preferred_element_type=f32)


def nt(a, b):
    return lax.dot_general(a, b, (((1,), (1,)), ((), ())), preferred_element_type=f32)


def factor_kernel(at_ref, scale_ref, own, other, theta, other_theta, out, squares, lh, ll, rh, rl, acc, dm, xs):
    n = own.shape[1]
    blocks = n // NB
    r = at_ref[2]
    i0 = lax.broadcasted_iota(jnp.int32, (NB, NB), 0)
    i1 = lax.broadcasted_iota(jnp.int32, (NB, NB), 1)
    lanes = lax.broadcasted_iota(jnp.int32, (NB, n), 1)
    eye = i0 == i1
    parts = jnp.zeros((NB, n), f32)
    for p in (own, other):
        for at in range(0, p.shape[0], NB):
            value = p[at : at + NB, :].astype(f32)
            parts = parts + value * value
    added = ridge_ratio * jnp.sum(parts) / r.astype(f32)

    def outer(j, carry):
        js = pl.multiple_of(j * NB, NB)
        for block in range(blocks):

            @pl.when(j == block)
            def _(at=block * NB):
                here = slice(at, at + NB)
                g = tn(own[:, here], own[:, at:]) + tn(other[:, here], other[:, at:])
                if at:
                    h, l = rh[:at, here], rl[:at, here]
                    g = g - (tn(h, rh[:at, at:]) + tn(h, rl[:at, at:]) + tn(l, rh[:at, at:]))
                    acc[:, :at] = -(tn(h, lh[:at, :at]) + tn(h, ll[:at, :at]) + tn(l, lh[:at, :at]))
                acc[:, at:] = g

        d = acc[:, pl.ds(js, NB)]
        dm[:, :NB] = d + jnp.where(eye, jnp.where(i0 + js < r, added, 1.0), 0.0)
        dm[:, NB:] = jnp.where(eye, 1.0, 0.0)
        diag_factor(dm, xs)
        inv = split(xs[:, NB:])
        row = nn3(inv, split(acc[...]))
        rh[pl.ds(js, NB), :], rl[pl.ds(js, NB), :] = split(row)
        lh[pl.ds(js, NB), :], ll[pl.ds(js, NB), :] = split(jnp.where(lanes < js, row, 0.0))
        lh[pl.ds(js, NB), pl.ds(js, NB)], ll[pl.ds(js, NB), pl.ds(js, NB)] = inv
        return carry

    lax.fori_loop(0, blocks, outer, 0)
    rows = out.shape[0]
    left = at_ref[0] == 0

    squares[...] = jnp.zeros(squares.shape, f32)

    @pl.when(left)
    def _():
        carried = jnp.dot(theta[...], own[...], preferred_element_type=f32) + jnp.dot(
            other_theta[...], other[...], preferred_element_type=f32
        )
        high, low = split(carried)
        upper = nt(high, lh[...]) + nt(low, lh[...]) + nt(high, ll[...])
        out[:, :n] = upper[:rows]
        out[:, n:] = upper[rows:]
        part = (upper * upper).reshape(-1, 8, n).sum(axis=0)
        part = sum(part[:, at : at + NB] for at in range(0, n, NB))
        for to in range(squares.shape[0]):
            squares[to] = part

    @pl.when(jnp.logical_not(left))
    def _():
        at = pl.multiple_of(at_ref[1] * rows, rows)
        both = jnp.concatenate([lh[pl.ds(at, rows), :], ll[pl.ds(at, rows), :]], 0)
        for q, half in enumerate((other, own)):
            value = nt(both, half[...])
            out[:, q * n : (q + 1) * n] = (value[:rows] + value[rows:]) * scale_ref[0]


def factored(place, scale, own, other, theta, other_theta):
    n = own.shape[1]
    rows = theta.shape[0] // 2
    count = lax.axis_size("y") * lax.axis_size("x")
    smem = pl.BlockSpec(memory_space=pltpu.SMEM)
    vmem = pl.BlockSpec(memory_space=pltpu.VMEM)
    return pl.pallas_call(
        factor_kernel,
        out_shape=(
            jax.ShapeDtypeStruct((rows, 2 * n), f32),
            jax.ShapeDtypeStruct((count, 8, NB), f32),
        ),
        in_specs=[smem, smem, vmem, vmem, vmem, vmem],
        out_specs=(vmem, vmem),
        scratch_shapes=[
            pltpu.VMEM((n, n), bf16),
            pltpu.VMEM((n, n), bf16),
            pltpu.VMEM((n, n), bf16),
            pltpu.VMEM((n, n), bf16),
            pltpu.VMEM((NB, n), f32),
            pltpu.VMEM((NB, 2 * NB), f32),
            pltpu.VMEM((NB, 2 * NB), f32),
        ],
        compiler_params=pltpu.CompilerParams(vmem_limit_bytes=32 * 2**20),
        cost_estimate=pl.CostEstimate(
            flops=20 * n**3, bytes_accessed=8 * n * n, transcendentals=n
        ),
    )(place, scale, own, other, theta, other_theta)


def other_core(value):
    return lax.ppermute(value, "core", [(0, 1), (1, 0)])


def gathered(value):
    count = lax.axis_size("y") * lax.axis_size("x")
    copies = jnp.broadcast_to(value[None], (count,) + value.shape)
    arrived = lax.all_to_all(copies, BOND, split_axis=0, concat_axis=0, tiled=True)
    return arrived.reshape(count * value.shape[0], value.shape[1])


def local(sites, start, gates, bonds):
    core = lax.axis_index("core")
    bond_index = lax.axis_index(BOND)
    is_left = core == 0
    width = start.shape[2]
    rows = sites.shape[1]
    left_site = 2 * lax.axis_index("z")
    bond_left = bonds[left_site]
    bond_mid = bonds[left_site + 1]
    bond_right = bonds[left_site + 2]
    columns = jnp.arange(width)
    mid_keep = columns < bond_mid
    right_keep = columns < bond_right
    row_keep = bond_index * rows + jnp.arange(rows) < bond_left
    own_site = sites[0]
    own_start = start[0]

    other_site = other_core(own_site)
    a_rows = jnp.where(is_left, own_site, other_site)
    b_rows = jnp.where(is_left, other_site[:, :width], own_site[:, width:])
    b_full = gathered(b_rows)
    start_full = gathered(own_start)

    keep = row_keep[:, None] & mid_keep[None, :]
    a_stack = jnp.concatenate(
        [jnp.where(keep, a_rows[:, i * width : (i + 1) * width], jnp.zeros((), bf16)) for i in (0, 1)], 0
    )
    mixed = jnp.where(right_keep[None, :], jnp.dot(a_stack, b_full, preferred_element_type=f32), 0.0)
    gate = gates[left_site].reshape(2, 2, 2, 2)
    gate = lax.dynamic_index_in_dim(gate, core, 3, keepdims=False)

    def mix(q):
        u = lax.dynamic_index_in_dim(gate, q, 1, keepdims=False)
        return jnp.concatenate(
            [u[o, 0] * mixed[:rows] + u[o, 1] * mixed[rows:] for o in (0, 1)], 0
        )

    theta = (mix(core) + other_core(mix(1 - core))).astype(bf16)
    other_theta, start_full = lax.optimization_barrier((other_core(theta), start_full))
    part = jnp.dot(theta, start_full, preferred_element_type=f32)
    image = jnp.where(mid_keep[None, :], part + other_core(part), 0.0).astype(bf16)
    terms = lax.dot_general(
        theta, image, (((0,), (0,)), ((), ())), preferred_element_type=f32
    ).astype(bf16)
    arrived = lax.all_to_all(
        terms.reshape(-1, rows, width), BOND, split_axis=0, concat_axis=0, tiled=True
    )
    projected = arrived.astype(f32).sum(axis=0).astype(bf16)
    own_half = gathered(projected)
    other_half = other_core(own_half)
    place = jnp.stack([core, bond_index, bond_mid])
    scale = jnp.sqrt(2.0 * bond_right.astype(f32))
    value, squares = factored(
        place, scale.reshape(1), own_half, other_half, theta, other_theta
    )
    total = jnp.sum(
        lax.all_to_all(squares, BOND, split_axis=0, concat_axis=0, tiled=True)
    )
    mean_square = total / (2.0 * bond_left.astype(f32) * bond_mid.astype(f32)) + 1e-06
    return (value * jnp.where(is_left, lax.rsqrt(mean_square), 1.0))[None]


def solution(mesh):
    chain, bond = mesh.shape["chain"], mesh.shape["bond"]
    side = 4
    torus = Mesh(
        mesh.devices.reshape(chain // 2, 2, bond // side, side), ("z", "core", "y", "x")
    )
    whole = P(("z", "core"), BOND, None)
    return jax.shard_map(
        local, mesh=torus, in_specs=(whole, whole, P(), P()), out_specs=whole, check_vma=False
    )
```

```python
import functools

import jax
import jax.numpy as jnp
from jax import lax
from jax.experimental import pallas as pl
from jax.experimental.pallas import tpu as pltpu
from jax.sharding import Mesh
from jax.sharding import PartitionSpec as P

BOND = ("y", "x")
NB = 128
SB = 32

ridge_ratio = 0.05
bf16 = jnp.bfloat16
f32 = jnp.float32


def split(x):
    high = x.astype(bf16)
    return high, (x - high.astype(f32)).astype(bf16)


def tn3(a, b):
    return lax.dot_general(
        jnp.concatenate([a[0], a[0], a[1]], 0),
        jnp.concatenate([b[0], b[1], b[0]], 0),
        (((0,), (0,)), ((), ())),
        preferred_element_type=f32,
    )


def nn3(a, b):
    return jnp.dot(
        jnp.concatenate([a[0], a[0], a[1]], 1),
        jnp.concatenate([b[0], b[1], b[0]], 0),
        preferred_element_type=f32,
    )


def diag_factor(dm, xs):
    groups = SB // 8
    tiles = range(2)
    for base in range(0, NB, SB):
        block = [dm[base + 8 * g : base + 8 * g + 8, :] for g in range(groups)]
        cols = {
            (m, g): jnp.broadcast_to(block[g][:, base + m : base + m + 1], (8, NB))
            for m in range(SB)
            for g in range(m // 8, groups)
        }
        rest = [[block[g][:, t * NB : (t + 1) * NB] for t in tiles] for g in range(groups)]
        for j in range(SB):
            first, sub = divmod(j, 8)
            rinv = lax.rsqrt(jnp.broadcast_to(cols[j, first][sub : sub + 1, :], (8, NB)))
            low = {g: cols[j, g] * rinv for g in range(first, groups)}
            done = [jnp.broadcast_to(rest[first][t][sub : sub + 1, :], (8, NB)) * rinv for t in tiles]
            for t in tiles:
                xs[base + j : base + j + 1, t * NB : (t + 1) * NB] = done[t][0:1, :]
            for m in range(j + 1, SB):
                factor = jnp.broadcast_to(low[m // 8][m % 8 : m % 8 + 1, :], (8, NB))
                for g in range(m // 8, groups):
                    cols[m, g] = cols[m, g] - low[g] * factor
            for g in range(first, groups):
                for t in tiles:
                    rest[g][t] = rest[g][t] - low[g] * done[t]
        end = base + SB
        if end < NB:
            high, rem = split(xs[base:end, :])
            u = tn3((high[:, :NB], rem[:, :NB]), (high, rem))
            dm[end:, :] = dm[end:, :] - u[end:]


def tn(a, b):
    return lax.dot_general(a, b, (((0,), (0,)), ((), ())), preferred_element_type=f32)


def nt(a, b):
    return lax.dot_general(a, b, (((1,), (1,)), ((), ())), preferred_element_type=f32)


def factor_kernel(at_ref, scale_ref, own, other, theta, other_theta, out, squares, lh, ll, rh, rl, acc, dm, xs):
    n = own.shape[1]
    blocks = n // NB
    r = at_ref[2]
    i0 = lax.broadcasted_iota(jnp.int32, (NB, NB), 0)
    i1 = lax.broadcasted_iota(jnp.int32, (NB, NB), 1)
    lanes = lax.broadcasted_iota(jnp.int32, (NB, n), 1)
    eye = i0 == i1
    parts = jnp.zeros((NB, n), f32)
    for p in (own, other):
        for at in range(0, p.shape[0], NB):
            value = p[at : at + NB, :].astype(f32)
            parts = parts + value * value
    added = ridge_ratio * jnp.sum(parts) / r.astype(f32)

    def outer(j, carry):
        js = pl.multiple_of(j * NB, NB)
        for block in range(blocks):

            @pl.when(j == block)
            def _(at=block * NB):
                here = slice(at, at + NB)
                g = tn(own[:, here], own[:, at:]) + tn(other[:, here], other[:, at:])
                if at:
                    h, l = rh[:at, here], rl[:at, here]
                    g = g - (tn(h, rh[:at, at:]) + tn(h, rl[:at, at:]) + tn(l, rh[:at, at:]))
                    acc[:, :at] = -(tn(h, lh[:at, :at]) + tn(h, ll[:at, :at]) + tn(l, lh[:at, :at]))
                acc[:, at:] = g

        d = acc[:, pl.ds(js, NB)]
        dm[:, :NB] = d + jnp.where(eye, jnp.where(i0 + js < r, added, 1.0), 0.0)
        dm[:, NB:] = jnp.where(eye, 1.0, 0.0)
        diag_factor(dm, xs)
        inv = split(xs[:, NB:])
        row = nn3(inv, split(acc[...]))
        rh[pl.ds(js, NB), :], rl[pl.ds(js, NB), :] = split(row)
        lh[pl.ds(js, NB), :], ll[pl.ds(js, NB), :] = split(jnp.where(lanes < js, row, 0.0))
        lh[pl.ds(js, NB), pl.ds(js, NB)], ll[pl.ds(js, NB), pl.ds(js, NB)] = inv
        return carry

    lax.fori_loop(0, blocks, outer, 0)
    rows = out.shape[0]
    left = at_ref[0] == 0

    squares[...] = jnp.zeros(squares.shape, f32)

    @pl.when(left)
    def _():
        carried = jnp.dot(theta[...], own[...], preferred_element_type=f32) + jnp.dot(
            other_theta[...], other[...], preferred_element_type=f32
        )
        high, low = split(carried)
        upper = nt(high, lh[...]) + nt(low, lh[...]) + nt(high, ll[...])
        out[:, :n] = upper[:rows]
        out[:, n:] = upper[rows:]
        part = (upper * upper).reshape(-1, 8, n).sum(axis=0)
        part = sum(part[:, at : at + NB] for at in range(0, n, NB))
        for to in range(squares.shape[0]):
            squares[to] = part

    @pl.when(jnp.logical_not(left))
    def _():
        at = pl.multiple_of(at_ref[1] * rows, rows)
        both = jnp.concatenate([lh[pl.ds(at, rows), :], ll[pl.ds(at, rows), :]], 0)
        for q, half in enumerate((other, own)):
            value = nt(both, half[...])
            out[:, q * n : (q + 1) * n] = (value[:rows] + value[rows:]) * scale_ref[0]


def factored(place, scale, own, other, theta, other_theta):
    n = own.shape[1]
    rows = theta.shape[0] // 2
    count = lax.axis_size("y") * lax.axis_size("x")
    smem = pl.BlockSpec(memory_space=pltpu.SMEM)
    vmem = pl.BlockSpec(memory_space=pltpu.VMEM)
    return pl.pallas_call(
        factor_kernel,
        out_shape=(
            jax.ShapeDtypeStruct((rows, 2 * n), f32),
            jax.ShapeDtypeStruct((count, 8, NB), f32),
        ),
        in_specs=[smem, smem, vmem, vmem, vmem, vmem],
        out_specs=(vmem, vmem),
        scratch_shapes=[
            pltpu.VMEM((n, n), bf16),
            pltpu.VMEM((n, n), bf16),
            pltpu.VMEM((n, n), bf16),
            pltpu.VMEM((n, n), bf16),
            pltpu.VMEM((NB, n), f32),
            pltpu.VMEM((NB, 2 * NB), f32),
            pltpu.VMEM((NB, 2 * NB), f32),
        ],
        compiler_params=pltpu.CompilerParams(vmem_limit_bytes=32 * 2**20),
        cost_estimate=pl.CostEstimate(
            flops=20 * n**3, bytes_accessed=8 * n * n, transcendentals=n
        ),
    )(place, scale, own, other, theta, other_theta)


def image_kernel(theta, start, part):
    value = jnp.dot(theta[...], start[...], preferred_element_type=f32)

    @pl.when(pl.program_id(0) == 0)
    def _():
        part[...] = value

    @pl.when(pl.program_id(0) > 0)
    def _():
        part[...] = part[...] + value


def image_part(theta, start):
    rows, n = theta.shape
    depth = 2 * NB
    return pl.pallas_call(
        image_kernel,
        grid=(n // depth,),
        out_shape=jax.ShapeDtypeStruct((rows, n), f32),
        in_specs=[
            pl.BlockSpec((rows, depth), lambda k: (0, k)),
            pl.BlockSpec((depth, n), lambda k: (k, 0)),
        ],
        out_specs=pl.BlockSpec((rows, n), lambda k: (0, 0)),
        compiler_params=pltpu.CompilerParams(vmem_limit_bytes=16 * 2**20),
        cost_estimate=pl.CostEstimate(
            flops=2 * rows * n * n, bytes_accessed=3 * n * n, transcendentals=0
        ),
    )(theta, start)


def other_core(value):
    return lax.ppermute(value, "core", [(0, 1), (1, 0)])


def gathered(value):
    count = lax.axis_size("y") * lax.axis_size("x")
    copies = jnp.broadcast_to(value[None], (count,) + value.shape)
    arrived = lax.all_to_all(copies, BOND, split_axis=0, concat_axis=0, tiled=True)
    return arrived.reshape(count * value.shape[0], value.shape[1])


def local(sites, start, gates, bonds):
    core = lax.axis_index("core")
    bond_index = lax.axis_index(BOND)
    is_left = core == 0
    width = start.shape[2]
    rows = sites.shape[1]
    left_site = 2 * lax.axis_index("z")
    bond_left = bonds[left_site]
    bond_mid = bonds[left_site + 1]
    bond_right = bonds[left_site + 2]
    columns = jnp.arange(width)
    mid_keep = columns < bond_mid
    right_keep = columns < bond_right
    row_keep = bond_index * rows + jnp.arange(rows) < bond_left
    own_site = sites[0]
    own_start = start[0]

    other_site = other_core(own_site)
    a_rows = jnp.where(is_left, own_site, other_site)
    b_rows = jnp.where(is_left, other_site[:, :width], own_site[:, width:])
    b_full = gathered(b_rows)
    start_full = gathered(own_start)

    keep = row_keep[:, None] & mid_keep[None, :]
    a_stack = jnp.concatenate(
        [jnp.where(keep, a_rows[:, i * width : (i + 1) * width], jnp.zeros((), bf16)) for i in (0, 1)], 0
    )
    mixed = jnp.where(right_keep[None, :], jnp.dot(a_stack, b_full, preferred_element_type=f32), 0.0)
    gate = gates[left_site].reshape(2, 2, 2, 2)
    gate = lax.dynamic_index_in_dim(gate, core, 3, keepdims=False)

    def mix(q):
        u = lax.dynamic_index_in_dim(gate, q, 1, keepdims=False)
        return jnp.concatenate(
            [u[o, 0] * mixed[:rows] + u[o, 1] * mixed[rows:] for o in (0, 1)], 0
        )

    theta = (mix(core) + other_core(mix(1 - core))).astype(bf16)
    other_theta, start_full = lax.optimization_barrier((other_core(theta), start_full))
    part = image_part(theta, start_full)
    image = jnp.where(mid_keep[None, :], part + other_core(part), 0.0).astype(bf16)
    terms = lax.dot_general(
        theta, image, (((0,), (0,)), ((), ())), preferred_element_type=f32
    ).astype(bf16)
    arrived = lax.all_to_all(
        terms.reshape(-1, rows, width), BOND, split_axis=0, concat_axis=0, tiled=True
    )
    projected = arrived.astype(f32).sum(axis=0).astype(bf16)
    own_half = gathered(projected)
    other_half = other_core(own_half)
    place = jnp.stack([core, bond_index, bond_mid])
    scale = jnp.sqrt(2.0 * bond_right.astype(f32))
    value, squares = factored(
        place, scale.reshape(1), own_half, other_half, theta, other_theta
    )
    total = jnp.sum(
        lax.all_to_all(squares, BOND, split_axis=0, concat_axis=0, tiled=True)
    )
    mean_square = total / (2.0 * bond_left.astype(f32) * bond_mid.astype(f32)) + 1e-06
    return (value * jnp.where(is_left, lax.rsqrt(mean_square), 1.0))[None]


def solution(mesh):
    chain, bond = mesh.shape["chain"], mesh.shape["bond"]
    side = 4
    torus = Mesh(
        mesh.devices.reshape(chain // 2, 2, bond // side, side), ("z", "core", "y", "x")
    )
    whole = P(("z", "core"), BOND, None)
    return jax.shard_map(
        local, mesh=torus, in_specs=(whole, whole, P(), P()), out_specs=whole, check_vma=False
    )
```
